32 devices in a mesh: ctx: 4 (over y, core), ep: 8 (over z, x).
Axes of the slice: x: 2, y: 2, z: 4, core: 2. Of those that a mesh axis runs over, the one named last changes fastest.
Arguments:
- queries: bfloat16 [16, 128, 576], P('ep'), may hold values from -52 to 52
- latent_cache: bfloat16 [16, 1024, 576], P('ep', 'ctx'), may hold values from -6 to 6
- lengths: int32 [16], P('ep'), may hold values from 32 to 1024, as said below
- value_up_weight: bfloat16 [128, 512, 128], P('ctx'), may hold values from -3 to 3
- out_proj: bfloat16 [16384, 7168], P('ctx', 'ep'), may hold values from -0.046875 to 0.046875
- residual: bfloat16 [16, 7168], P('ctx', 'ep'), may hold values from -41 to 41
- norm_gain: bfloat16 [7168], P('ep'), may hold values from 0.5 to 1.5
- expert_ids: int32 [16, 2], replicated, may hold values from 0 to 3, all different within a row; in each aligned block of 16 rows (0 to 15, 16 to 31, ...) at most 12 rows name the same one
- expert_route_weight: float32 [16, 2], replicated, may hold values from 0.1 to 0.5
- gate_proj: bfloat16 [4, 7168, 1024], P('ctx', 'ep'), may hold values from -0.0625 to 0.0625
- up_proj: bfloat16 [4, 7168, 1024], P('ctx', 'ep'), may hold values from -0.0625 to 0.0625
- down_proj: bfloat16 [4, 1024, 7168], P('ctx', None, 'ep'), may hold values from -0.1875 to 0.1875
Outputs:
- layer_out: bfloat16 [16, 7168], P('ctx', 'ep')
The draws below stay inside these ranges and needn't reach their ends.
Inputs may be any that keep to these rules, and one draw needn't show every extreme that they name: `lengths`: some row has length 1024. `expert_ids`: each row names 2 different experts; no expert is named by more than 12 rows, a bound that some block reaches.
All inputs are finite; a program needn't handle non-finite values.
Results may differ from the reference program's by a relative error of at most 0.0064.
Values may be sent and summed in bfloat16 or wider, within the bound.
A program may use at most 64 MiB of HBM per device.

```python
import math
import jax
import jax.numpy as jnp
import numpy as np
from jax import lax

D = 7168
HEADS = 128
LATENT = 512
ROPE = 64
VDIM = 128
FFW = 1024
CTX_DEV = 256
ROWS = 16
CONTEXT = 1024
EXPERTS = 4
TOP = 2
CAPACITY = 12
N_CTX = 4


def draw_queries(key, part):
    key = jax.random.fold_in(key, 12)
    width = LATENT + ROPE
    values = jnp.clip(jax.random.normal(key, (ROWS, HEADS, width), jnp.float32), -6.0, 6.0)
    return values.astype(jnp.bfloat16)


def draw_latent_cache(key, part):
    key = jax.random.fold_in(key, 11)
    width = LATENT + ROPE
    values = jnp.clip(jax.random.normal(key, (ROWS, CONTEXT, width), jnp.float32), -6.0, 6.0)
    return values.astype(jnp.bfloat16)


def draw_lengths(key, part):
    key = jax.random.fold_in(key, 5)
    drawn = jax.random.randint(key, (ROWS,), CONTEXT // 32, CONTEXT + 1)
    longest = jax.random.randint(jax.random.fold_in(key, 1), (), 0, ROWS)
    return drawn.at[longest].set(CONTEXT).astype(jnp.int32)


def draw_residual(key, part):
    key = jax.random.fold_in(key, 3)
    values = jnp.clip(jax.random.normal(key, (ROWS, D), jnp.float32), -4.0, 4.0)
    return values.astype(jnp.bfloat16)


def block_scale(rng, extent, split, low, top_value):
    def one(dim, shards_of):
        steps = jax.random.uniform(jax.random.fold_in(jax.random.fold_in(rng, 6), dim), (shards_of,), jnp.float32, low / len(split), top_value / len(split))
        return jnp.repeat(jnp.exp(steps), extent[dim] // shards_of).reshape((-1,) + (1,) * (len(extent) - dim - 1))

    level = one(*split[0])
    for cut in split[1:]:
        level = level * one(*cut)
    return level


def deal_out(key, own, number, rows, count, top, most, skew):
    sequence = jax.random.permutation(key, count)
    heavy_load, common = shares(count, rows * top, most, skew, True), shares(count, rows * top, most, skew, False)
    places = jnp.arange(count)

    def named(sizes, rotation):
        used = int((sizes > 0).sum())
        fixed = max(1, used // 4)
        passed = fixed + (places - fixed + rotation * (used - fixed)) % max(1, count - fixed)
        return jnp.zeros((count,), jnp.int32).at[sequence[jnp.where(places < fixed, places, passed)]].set(jnp.asarray(sizes, jnp.int32))

    sizes = jnp.where(number % 4 == 0, named(heavy_load, number // 4), named(common, number - number // 4 - 1))
    mixed = jax.random.permutation(jax.random.fold_in(own, 3), count)
    source_of, receiver = mixed[0:count // 2 * 2:2], mixed[1:count // 2 * 2:2]
    room = jnp.minimum(sizes[source_of] - 1, most - sizes[receiver]) // 2
    room = jnp.where((source_of == sequence[0]) | (receiver == sequence[0]) | (sizes[receiver] == 0), 0, jnp.maximum(room, 0))
    passed = jax.random.randint(jax.random.fold_in(own, 4), (count // 2,), 0, 1 << 20) % (room + 1)
    sizes = sizes.at[source_of].add(-passed).at[receiver].add(passed)
    items = jnp.searchsorted(jnp.cumsum(sizes), jnp.arange(rows * top), side="right").astype(jnp.int32)
    grid = items.reshape(top, rows).T
    grid = grid[jax.random.permutation(jax.random.fold_in(own, 1), rows)]
    rotation = jax.random.randint(jax.random.fold_in(own, 2), (rows, 1), 0, top)
    return jnp.take_along_axis(grid, (jnp.arange(top)[None, :] + rotation) % top, axis=1)


def shares(amount, total, most, slope, full):
    loads = [(1 << 20) // math.isqrt(grade ** slope) + 1 for grade in range(1, amount + 1)]
    largest = most if full else min(most, max(-(-total // amount), total * loads[0] // sum(loads)))
    least = 1 if total - largest >= amount - 1 else 0
    holding, rest = [largest] + [least] * (amount - 1), total - largest - least * (amount - 1)
    while rest > 0:
        free = [i for i in range(1, amount) if holding[i] < largest] or [i for i in range(1, amount) if holding[i] < most]
        mass, left = sum([loads[i] for i in free]), rest
        for i in free:
            addition = min(most - holding[i], max(1, left * loads[i] // mass), rest)
            holding[i] = holding[i] + addition
            rest = rest - addition
    return np.array(holding)


def noise(stream_key, dims, deviation, most, split=(), kind=jnp.bfloat16):
    values = deviation * jax.random.normal(stream_key, dims, jnp.float32)
    if split:
        values = values * block_scale(stream_key, dims, split, -0.22, 0.18)
    return jnp.clip(values, -most, most).astype(kind)


def setup_inputs(seed: int = 0) -> dict:
    key_of = jax.random.split(jax.random.key(seed), 13)
    queries = draw_queries(jax.random.fold_in(key_of[12], 71), 0)
    latent_cache = draw_latent_cache(jax.random.fold_in(key_of[12], 71), 0)
    lengths = draw_lengths(jax.random.fold_in(key_of[12], 71), 0)
    value_up_weight = noise(key_of[3], (HEADS, LATENT, VDIM), 4 ** -0.5, 3.0, ((0, 4),))
    out_proj = noise(key_of[4], (HEADS * VDIM, D), (HEADS * VDIM) ** -0.5, 0.046875, ((0, 4), (1, 8)))
    residual = draw_residual(jax.random.fold_in(key_of[12], 71), 0)
    norm_gain = jnp.clip(1.0 + 0.1 * jax.random.normal(key_of[6], (D,), jnp.float32), 0.5, 1.5).astype(jnp.bfloat16)
    expert_ids_keys = jax.random.split(jax.random.fold_in(key_of[7], 1), ROWS // ROWS)
    expert_ids_turns = jax.random.permutation(jax.random.fold_in(key_of[7], 3), ROWS // ROWS)
    expert_ids = jax.vmap(lambda own, number: deal_out(jax.random.fold_in(key_of[7], 2), own, number, ROWS, EXPERTS, TOP, CAPACITY, 2))(expert_ids_keys, expert_ids_turns).reshape((ROWS, TOP))
    expert_route_weight = jnp.clip(jax.random.uniform(key_of[8], (ROWS, TOP), jnp.float32, 0.1, 0.5), 0.1, 0.5)
    gate_proj = noise(key_of[9], (EXPERTS, D, FFW), D ** -0.5, 0.0625, ((0, 4), (1, 8)))
    up_proj = noise(key_of[10], (EXPERTS, D, FFW), D ** -0.5, 0.0625, ((0, 4), (1, 8)))
    down_proj = noise(key_of[11], (EXPERTS, FFW, D), FFW ** -0.5, 0.1875, ((0, 4), (2, 8)))
    return dict(queries=queries, latent_cache=latent_cache, lengths=lengths, value_up_weight=value_up_weight, out_proj=out_proj, residual=residual, norm_gain=norm_gain, expert_ids=expert_ids, expert_route_weight=expert_route_weight, gate_proj=gate_proj, up_proj=up_proj, down_proj=down_proj)


SOFTMAX_SCALE = 192.0 ** (-0.5)
EPSILON = 1e-06

def merge_parts(earlier, later):
    left_running_max, total_left, left_numerator = earlier
    peak_right, total_right, numer_right = later
    top_score = jnp.maximum(left_running_max, peak_right)
    factor_left = jnp.exp(left_running_max - top_score)
    factor_right = jnp.exp(peak_right - top_score)
    totals = total_left * factor_left + total_right * factor_right
    numerator = left_numerator * factor_left[..., None] + numer_right * factor_right[..., None]
    return (top_score, totals, numerator)

def reference(queries, latent_cache, lengths, value_up_weight, out_proj, residual, norm_gain, expert_ids, expert_route_weight, gate_proj, up_proj, down_proj):
    queries_wide = queries.astype(jnp.float32)

    def block_step(carry, block_index):
        start_pos = block_index * CTX_DEV
        keys_block = lax.dynamic_slice_in_dim(latent_cache, start_pos, CTX_DEV, 1).astype(jnp.float32)
        scores = jnp.einsum('rhk,rpk->rhp', queries_wide, keys_block) * SOFTMAX_SCALE
        positions = start_pos + jnp.arange(CTX_DEV, dtype=jnp.int32)
        is_valid = (positions[None, :] < lengths[:, None])[:, None, :]
        masked = jnp.where(is_valid, scores, -1e+30)
        top_score = lax.optimization_barrier(jnp.max(masked, axis=-1))
        weights = jnp.where(is_valid, jnp.exp(masked - top_score[..., None]), 0.0)
        totals = lax.optimization_barrier(jnp.sum(weights, axis=-1))
        rounded = lax.optimization_barrier(weights.astype(jnp.bfloat16)).astype(jnp.float32)
        numerator = jnp.einsum('rhp,rpk->rhk', rounded, keys_block[:, :, :LATENT])
        return (merge_parts(carry, (top_score, totals, numerator)), None)
    start_state = (jnp.full((ROWS, HEADS), -1e+30, jnp.float32), jnp.zeros((ROWS, HEADS), jnp.float32), jnp.zeros((ROWS, HEADS, LATENT), jnp.float32))
    merged, unused = lax.scan(block_step, start_state, jnp.arange(N_CTX, dtype=jnp.int32))
    top_score, totals, numerator = merged
    attention_result = lax.optimization_barrier((numerator / totals[..., None]).astype(jnp.bfloat16))
    value_per_head = jnp.einsum('dxp,xpz->dxz', attention_result.astype(jnp.float32), value_up_weight.astype(jnp.float32))
    value_per_head = value_per_head.astype(jnp.bfloat16).reshape(ROWS, HEADS * VDIM)
    attn_out = jnp.dot(value_per_head, out_proj, preferred_element_type=jnp.float32)
    hidden_in = lax.optimization_barrier((residual.astype(jnp.float32) + attn_out).astype(jnp.bfloat16))
    hidden_wide = hidden_in.astype(jnp.float32)
    inv_rms = lax.rsqrt(lax.optimization_barrier(jnp.mean(hidden_wide * hidden_wide, axis=-1)) + EPSILON)
    normed = (hidden_wide * norm_gain.astype(jnp.float32)).astype(jnp.bfloat16)

    def expert_step(moe_sum, expert_index):
        gate = inv_rms[:, None] * jnp.dot(normed, gate_proj[expert_index], preferred_element_type=jnp.float32)
        upper = inv_rms[:, None] * jnp.dot(normed, up_proj[expert_index], preferred_element_type=jnp.float32)
        expert_hidden = (jax.nn.silu(gate) * upper).astype(jnp.bfloat16)
        expert_out = jnp.dot(expert_hidden, down_proj[expert_index], preferred_element_type=jnp.float32)
        row_weight = lax.optimization_barrier(jnp.sum(jnp.where(expert_ids == expert_index, expert_route_weight, 0.0), axis=1))
        return (moe_sum + row_weight[:, None] * expert_out, None)
    moe_sum, unused = lax.scan(expert_step, jnp.zeros((ROWS, D), jnp.float32), jnp.arange(EXPERTS, dtype=jnp.int32))
    return (hidden_wide + moe_sum).astype(jnp.bfloat16)
```

```python
import functools

import jax
import jax.numpy as jnp
from jax import lax
from jax.experimental import pallas as pl
from jax.experimental.pallas import tpu as pltpu
from jax.sharding import PartitionSpec as P

LATENT = 512
VDIM = 128
LANES = 128
GROUP = 8
SOFTMAX_SCALE = 192.0 ** (-0.5)
EPSILON = 1e-06
MESH = pl.DeviceIdType.MESH
BF16 = jnp.bfloat16
F32 = jnp.float32


def remote(src, dst, send_sem, recv_sem, axis, peer):
    return pltpu.make_async_remote_copy(
        src_ref=src,
        dst_ref=dst,
        send_sem=send_sem,
        recv_sem=recv_sem,
        device_id={axis: peer},
        device_id_type=MESH,
    )


def total_of(parts):
    result = parts[0]
    for part in parts[1:]:
        result = result + part
    return result


def kernel(
    nc, ne, chunks,
    q_hbm, kv_hbm, len_ref, vup_hbm, wo_hbm, res_ref, gain_ref, ids_ref, rw_ref, wg_hbm, wu_hbm, wd_hbm,
    out_ref,
    q_v, kv_v, vup_v, wo_v, wg_v, wu_v, wd_v,
    num_s, num_r, st_s, st_r, hv_r, ao_r, hid_s, sq_s, sq_r, gu_s, gu_r, eh_r, mo_s, mo_r,
    row_sem, vup_sem, wo_sem, ffn_sem,
    num_ss, num_rs, st_ss, st_rs, hv_ss, hv_rs, ao_ss, ao_rs,
    sq_ss, sq_rs, gu_ss, gu_rs, eh_ss, eh_rs, mo_ss, mo_rs,
):
    c = lax.axis_index("ctx")
    e = lax.axis_index("ep")
    rl, heads, _ = q_v.shape
    positions = kv_v.shape[1]
    hpd = vup_v.shape[0]
    nq = hpd // GROUP
    qw = nq // chunks
    rows = ao_r.shape[1]
    dl = ao_r.shape[2]
    ro = rows // nc
    ffw = wg_v.shape[1]
    blocks = ffw // LANES
    gr = gu_s.shape[1]

    ctx_to = [lax.rem(c + d, nc) for d in range(1, nc)]
    ctx_from = [lax.rem(c + nc - d, nc) for d in range(1, nc)]
    ep_to = [lax.rem(e + d, ne) for d in range(1, ne)]
    ep_from = [lax.rem(e + ne - d, ne) for d in range(1, ne)]

    row_copies = []
    for r in range(rl):
        pair = (
            pltpu.make_async_copy(q_hbm.at[r], q_v.at[r], row_sem.at[r, 0]),
            pltpu.make_async_copy(kv_hbm.at[r], kv_v.at[r], row_sem.at[r, 1]),
        )
        row_copies.append(pair)
        for copy in pair:
            copy.start()

    barrier = pltpu.get_barrier_semaphore()
    for peer in ctx_to:
        pl.semaphore_signal(barrier, inc=1, device_id={"ctx": peer}, device_id_type=MESH)
    for peer in ep_to:
        pl.semaphore_signal(barrier, inc=1, device_id={"ep": peer}, device_id_type=MESH)

    vup_copies, wo_copies = [], []
    for ch in range(chunks):
        some = pl.ds(ch * qw * GROUP, qw * GROUP)
        vup_copies.append(pltpu.make_async_copy(vup_hbm.at[some], vup_v.at[some], vup_sem.at[ch]))
        vup_copies[-1].start()
    for ch in range(chunks):
        some = pl.ds(ch * qw * GROUP * VDIM, qw * GROUP * VDIM)
        wo_copies.append(pltpu.make_async_copy(wo_hbm.at[some], wo_v.at[some], wo_sem.at[ch]))
        wo_copies[-1].start()
    ffn_copies = [
        pltpu.make_async_copy(wg_hbm.at[0], wg_v, ffn_sem.at[0]),
        pltpu.make_async_copy(wu_hbm.at[0], wu_v, ffn_sem.at[1]),
        pltpu.make_async_copy(wd_hbm.at[0], wd_v, ffn_sem.at[2]),
    ]
    for copy in ffn_copies:
        copy.start()

    sends = []

    width = LANES // (2 * rl)
    stat_lane = lax.broadcasted_iota(jnp.int32, (heads, LANES), 1)
    place = c * positions + lax.broadcasted_iota(jnp.int32, (heads, positions), 1)
    stats = jnp.zeros((heads, LANES), F32)
    for r in range(rl):
        for copy in row_copies[r]:
            copy.wait()
        scores = lax.dot_general(
            q_v[r], kv_v[r], (((1,), (1,)), ((), ())), preferred_element_type=F32
        ) * SOFTMAX_SCALE
        valid = place < len_ref[r]
        masked = jnp.where(valid, scores, -1e30)
        top = jnp.max(masked, axis=1, keepdims=True)
        weights = jnp.where(valid, jnp.exp(masked - top), 0.0)
        total = jnp.sum(weights, axis=1, keepdims=True)
        numer = jnp.dot(weights.astype(BF16), kv_v[r, :, :LATENT], preferred_element_type=F32)
        for j in range(nc):
            num_s[j, r] = numer[j * hpd : (j + 1) * hpd].astype(BF16)
        stats = jnp.where(stat_lane >= 2 * r * width, top, stats)
        stats = jnp.where(stat_lane >= (2 * r + 1) * width, total, stats)
        if r == 0:
            pl.semaphore_wait(barrier, nc + ne - 2)
        if r == rl - 1:
            for j in range(nc):
                st_s[j] = stats[j * hpd : (j + 1) * hpd]
            for peer in ctx_to:
                sends.append(remote(st_s.at[peer], st_r.at[c], st_ss.at[peer], st_rs.at[c], "ctx", peer))
                sends[-1].start()
        for peer in ctx_to:
            sends.append(
                remote(num_s.at[peer, r], num_r.at[c, r], num_ss.at[peer, r], num_rs.at[c, r], "ctx", peer)
            )
            sends[-1].start()

    wide = rl * GROUP
    goal = lax.broadcasted_iota(jnp.int32, (rows * GROUP, ne * wide), 0)
    have = lax.broadcasted_iota(jnp.int32, (rows * GROUP, ne * wide), 1)
    target = (
        (have & (GROUP - 1)) * rows
        + lax.shift_right_logical(have, wide.bit_length() - 1) * rl
        + (lax.shift_right_logical(have, GROUP.bit_length() - 1) & (rl - 1))
    )
    shuffle = jnp.where(goal == target, 1.0, 0.0).astype(BF16)

    for src in ctx_from:
        remote(st_s.at[src], st_r.at[src], st_ss.at[src], st_rs.at[src], "ctx", src).wait_recv()
    for r in range(rl):
        for src in ctx_from:
            remote(num_s.at[src, r], num_r.at[src, r], num_ss.at[src, r], num_rs.at[src, r], "ctx", src).wait_recv()
    all_stats = [st_s[c]] + [st_r[src] for src in ctx_from]
    factors = []
    for r in range(rl):
        tops = [s[:, 2 * r * width : 2 * r * width + 1] for s in all_stats]
        totals = [s[:, (2 * r + 1) * width : (2 * r + 1) * width + 1] for s in all_stats]
        best = functools.reduce(jnp.maximum, tops)
        scale = [jnp.exp(t - best) for t in tops]
        whole = 1.0 / total_of([t * s for t, s in zip(totals, scale)])
        factors.append([s * whole for s in scale])
    row_of_group = lax.broadcasted_iota(jnp.int32, (wide, LATENT), 0) & (GROUP - 1)
    for ch in range(chunks):
        first = ch * qw * GROUP
        merged = []
        for r in range(rl):
            some = slice(first, first + qw * GROUP)
            parts = [num_s[c, r, some]] + [num_r[src, r, some] for src in ctx_from]
            merged.append(
                total_of([p.astype(F32) * f[some] for p, f in zip(parts, factors[r])])
            )
        vup_copies[ch].wait()
        values = []
        for q in range(qw):
            left = jnp.concatenate([m[q * GROUP : (q + 1) * GROUP] for m in merged], axis=0)
            left = jnp.concatenate(
                [jnp.where(row_of_group == g, left, 0.0).astype(BF16) for g in range(GROUP)], axis=1
            )
            right = vup_v[first + q * GROUP : first + (q + 1) * GROUP].reshape(GROUP * LATENT, VDIM)
            values.append(jnp.dot(left, right, preferred_element_type=F32).astype(BF16))
        hv_r[ch, e] = jnp.concatenate(values, axis=1) if qw > 1 else values[0]
        for peer in ep_to:
            sends.append(
                remote(hv_r.at[ch, e], hv_r.at[ch, e], hv_ss.at[ch, peer], hv_rs.at[ch, e], "ep", peer)
            )
            sends[-1].start()

    attn = None
    for ch in range(chunks):
        for src in ep_from:
            remote(hv_r.at[ch, src], hv_r.at[ch, src], hv_ss.at[ch, src], hv_rs.at[ch, src], "ep", src).wait_recv()
        came = hv_r[ch].reshape(ne * wide, qw * VDIM)
        sorted_values = jnp.dot(shuffle, came, preferred_element_type=F32).astype(BF16)
        left = jnp.concatenate(
            [
                sorted_values[g * rows : (g + 1) * rows, q * VDIM : (q + 1) * VDIM]
                for q in range(qw)
                for g in range(GROUP)
            ],
            axis=1,
        )
        wo_copies[ch].wait()
        depth = qw * GROUP * VDIM
        part = jnp.dot(left, wo_v[ch * depth : (ch + 1) * depth, :], preferred_element_type=F32)
        attn = part if attn is None else attn + part
    own_rows = lax.broadcasted_iota(jnp.int32, (rows, dl), 0) - c * ro
    spread = jnp.concatenate([res_ref[...].astype(F32)] * nc, axis=0)
    attn = attn + jnp.where((own_rows >= 0) & (own_rows < ro), spread, 0.0)
    ao_r[c] = attn.astype(BF16)
    for peer in ctx_to:
        sends.append(remote(ao_r.at[c], ao_r.at[c], ao_ss.at[peer], ao_rs.at[c], "ctx", peer))
        sends[-1].start()
    for src in ctx_from:
        remote(ao_r.at[src], ao_r.at[src], ao_ss.at[src], ao_rs.at[src], "ctx", src).wait_recv()
        attn = attn + ao_r[src].astype(F32)

    hidden = attn.astype(BF16).astype(F32)
    for j in range(nc):
        hid_s[j] = hidden[j * ro : (j + 1) * ro]
    square = jnp.sum(hidden * hidden, axis=1, keepdims=True)
    high = square.astype(BF16).astype(F32)
    sq_lane = lax.broadcasted_iota(jnp.int32, (rows, LANES), 1)
    both = jnp.where(sq_lane < LANES // 2, high, square - high).astype(BF16)
    for j in range(rows // gr):
        sq_s[j] = both[j * gr : (j + 1) * gr]
    for peer in ep_to:
        sends.append(
            remote(sq_s.at[peer // blocks], sq_r.at[e], sq_ss.at[peer], sq_rs.at[e], "ep", peer)
        )
        sends[-1].start()
    normed = (hidden * gain_ref[...].astype(F32)).astype(BF16)
    ffn_copies[0].wait()
    gate = jnp.dot(normed, wg_v[...], preferred_element_type=F32)
    ffn_copies[1].wait()
    upper = jnp.dot(normed, wu_v[...], preferred_element_type=F32)
    for p in range(ne):
        some = slice(p // blocks * gr, (p // blocks + 1) * gr)
        cols = slice(p % blocks * LANES, (p % blocks + 1) * LANES)
        gu_s[p] = jnp.concatenate([gate[some, cols], upper[some, cols]], axis=1).astype(BF16)
    for peer in ep_to:
        sends.append(remote(gu_s.at[peer], gu_r.at[e], gu_ss.at[peer], gu_rs.at[e], "ep", peer))
        sends[-1].start()
    squares = sq_s[e // blocks].astype(F32)
    sums = gu_s[e].astype(F32)
    for src in ep_from:
        remote(sq_s.at[0], sq_r.at[src], sq_ss.at[src], sq_rs.at[src], "ep", src).wait_recv()
        squares = squares + sq_r[src].astype(F32)
    for src in ep_from:
        remote(gu_s.at[src], gu_r.at[src], gu_ss.at[src], gu_rs.at[src], "ep", src).wait_recv()
        sums = sums + gu_r[src].astype(F32)
    square = squares[:, :1] + squares[:, LANES // 2 : LANES // 2 + 1]
    inv_rms = lax.rsqrt(square / (dl * ne) + EPSILON)
    gate = inv_rms * sums[:, :LANES]
    upper = inv_rms * sums[:, LANES:]
    eh_r[e] = (gate / (1.0 + jnp.exp(-gate)) * upper).astype(BF16)
    for peer in ep_to:
        sends.append(remote(eh_r.at[e], eh_r.at[e], eh_ss.at[peer], eh_rs.at[e], "ep", peer))
        sends[-1].start()
    route = jnp.sum(jnp.where(ids_ref[...] == c, rw_ref[...], 0.0), axis=1, keepdims=True)
    ffn_copies[2].wait()
    for src in ep_from:
        remote(eh_r.at[src], eh_r.at[src], eh_ss.at[src], eh_rs.at[src], "ep", src).wait_recv()

    left = [
        jnp.concatenate([eh_r[j * blocks + b] for b in range(blocks)], axis=1) for j in range(rows // gr)
    ]
    left = jnp.concatenate(left, axis=0) if len(left) > 1 else left[0]
    expert = route * jnp.dot(left, wd_v[...], preferred_element_type=F32)
    for j in range(nc):
        mo_s[j] = expert[j * ro : (j + 1) * ro]
    for peer in ctx_to:
        sends.append(remote(mo_s.at[peer], mo_r.at[c], mo_ss.at[peer], mo_rs.at[c], "ctx", peer))
        sends[-1].start()
    result = hid_s[c] + mo_s[c]
    for src in ctx_from:
        remote(mo_s.at[src], mo_r.at[src], mo_ss.at[src], mo_rs.at[src], "ctx", src).wait_recv()
        result = result + mo_r[src]
    out_ref[...] = result.astype(BF16)
    for copy in sends:
        copy.wait_send()


def local(
    nc, ne, queries, latent_cache, lengths, value_up, out_proj, residual, norm_gain,
    expert_ids, route_weight, gate_proj, up_proj, down_proj,
):
    rl, heads, width = queries.shape
    positions = latent_cache.shape[1]
    hpd = value_up.shape[0]
    ro, dl = residual.shape
    rows = expert_ids.shape[0]
    ffw = gate_proj.shape[2]
    blocks = ffw // LANES
    gr = rows * blocks // ne
    nq = hpd // GROUP
    chunks = 2 if nq % 2 == 0 else 1
    qw = nq // chunks
    wide = rl * GROUP
    vm = pltpu.VMEM
    dma = pltpu.SemaphoreType.DMA
    scratch = [
        vm((rl, heads, width), BF16),
        vm((rl, positions, width), BF16),
        vm(value_up.shape, BF16),
        vm(out_proj.shape, BF16),
        vm(gate_proj.shape[1:], BF16),
        vm(up_proj.shape[1:], BF16),
        vm(down_proj.shape[1:], BF16),
        vm((nc, rl, hpd, LATENT), BF16),
        vm((nc, rl, hpd, LATENT), BF16),
        vm((nc, hpd, LANES), F32),
        vm((nc, hpd, LANES), F32),
        vm((chunks, ne, wide, qw * VDIM), BF16),
        vm((nc, rows, dl), BF16),
        vm((nc, ro, dl), F32),
        vm((rows // gr, gr, LANES), BF16),
        vm((ne, gr, LANES), BF16),
        vm((ne, gr, 2 * LANES), BF16),
        vm((ne, gr, 2 * LANES), BF16),
        vm((ne, gr, LANES), BF16),
        vm((nc, ro, dl), F32),
        vm((nc, ro, dl), F32),
        dma((rl, 2)),
        dma((chunks,)),
        dma((chunks,)),
        dma((3,)),
    ]
    for shape in ((nc, rl), (nc,), (chunks, ne), (nc,), (ne,), (ne,), (ne,), (nc,)):
        scratch += [dma(shape), dma(shape)]
    held = pl.BlockSpec(memory_space=pltpu.VMEM)
    far = pl.BlockSpec(memory_space=pl.ANY)
    weights = value_up.size + out_proj.size + gate_proj.size + up_proj.size + down_proj.size
    return pl.pallas_call(
        functools.partial(kernel, nc, ne, chunks),
        out_shape=jax.ShapeDtypeStruct((ro, dl), BF16),
        in_specs=[
            far, far, pl.BlockSpec(memory_space=pltpu.SMEM), far, far, held, held, held, held, far, far, far,
        ],
        out_specs=held,
        scratch_shapes=scratch,
        compiler_params=pltpu.CompilerParams(
            collective_id=0, has_side_effects=True, vmem_limit_bytes=52 * 2**20
        ),
        cost_estimate=pl.CostEstimate(
            flops=2 * rows * weights, bytes_accessed=2 * weights, transcendentals=rl * heads * positions
        ),
        name="decode_step",
    )(
        queries, latent_cache, lengths, value_up, out_proj, residual, norm_gain.reshape(1, -1),
        expert_ids, route_weight, gate_proj, up_proj, down_proj,
    )


def solution(mesh):
    placed = (
        P("ep", None, None),
        P("ep", "ctx", None),
        P("ep"),
        P("ctx", None, None),
        P("ctx", "ep"),
        P("ctx", "ep"),
        P("ep"),
        P(),
        P(),
        P("ctx", "ep", None),
        P("ctx", "ep", None),
        P("ctx", None, "ep"),
    )
    step = functools.partial(local, mesh.shape["ctx"], mesh.shape["ep"])
    return jax.shard_map(step, mesh=mesh, in_specs=placed, out_specs=P("ctx", "ep"), check_vma=False)
```

```python
import functools

import jax
import jax.numpy as jnp
from jax import lax
from jax.experimental import pallas as pl
from jax.experimental.pallas import tpu as pltpu
from jax.sharding import PartitionSpec as P

LATENT = 512
VDIM = 128
LANES = 128
GROUP = 8
SOFTMAX_SCALE = 192.0 ** (-0.5)
EPSILON = 1e-06
MESH = pl.DeviceIdType.MESH
BF16 = jnp.bfloat16
F32 = jnp.float32


def remote(src, dst, send_sem, recv_sem, axis, peer):
    return pltpu.make_async_remote_copy(
        src_ref=src,
        dst_ref=dst,
        send_sem=send_sem,
        recv_sem=recv_sem,
        device_id={axis: peer},
        device_id_type=MESH,
    )


def flipped(index, bits):
    result, bit = index, 1
    while bit <= bits:
        if bits & bit:
            result = result + bit - 2 * bit * lax.rem(lax.div(index, bit), 2)
        bit *= 2
    return result


def total_of(parts):
    result = parts[0]
    for part in parts[1:]:
        result = result + part
    return result


def kernel(
    nc, ne, chunks,
    q_hbm, kv_hbm, len_hbm, vup_hbm, wo_hbm, res_hbm, gain_hbm, ids_hbm, rw_hbm, wg_hbm, wu_hbm, wd_hbm,
    out_ref,
    q_v, kv_v, vup_v, wo_v, wg_v, wu_v, wd_v, len_ref, res_ref, gain_ref, ids_ref, rw_ref,
    num_s, num_r, st_s, st_r, hv_r, ao_r, hid_s, sq_s, sq_r, gu_s, gu_r, eh_r, mo_s, mo_r,
    row_sem, vup_sem, wo_sem, ffn_sem, small_sem,
    num_ss, num_rs, st_ss, st_rs, hv_ss, hv_rs, ao_ss, ao_rs,
    sq_ss, sq_rs, gu_ss, gu_rs, eh_ss, eh_rs, mo_ss, mo_rs,
):
    c = lax.axis_index("ctx")
    e = lax.axis_index("ep")
    rl, _, heads = q_v.shape
    positions = kv_v.shape[2]
    hpd = vup_v.shape[0]
    nq = hpd // GROUP
    qw = nq // chunks
    rows = ao_r.shape[1]
    dl = ao_r.shape[2]
    ro = rows // nc
    ffw = wg_v.shape[1]
    blocks = ffw // LANES
    gr = gu_s.shape[1]

    ctx_peers = [flipped(c, bits) for bits in reversed(range(1, nc))]
    ep_peers = [flipped(e, bits) for bits in reversed(range(1, ne))]

    small_copies = [
        pltpu.make_async_copy(src, dst, small_sem.at[k])
        for k, (src, dst) in enumerate(
            ((len_hbm, len_ref), (res_hbm, res_ref), (gain_hbm, gain_ref), (ids_hbm, ids_ref), (rw_hbm, rw_ref))
        )
    ]
    small_copies[0].start()
    row_copies = []
    for r in range(rl):
        pair = (
            pltpu.make_async_copy(q_hbm.at[r], q_v.at[r], row_sem.at[r, 0]),
            pltpu.make_async_copy(kv_hbm.at[r], kv_v.at[r], row_sem.at[r, 1]),
        )
        row_copies.append(pair)
        for copy in pair:
            copy.start()

    barrier = pltpu.get_barrier_semaphore()
    for peer in ctx_peers:
        pl.semaphore_signal(barrier, inc=1, device_id={"ctx": peer}, device_id_type=MESH)
    for peer in ep_peers:
        pl.semaphore_signal(barrier, inc=1, device_id={"ep": peer}, device_id_type=MESH)

    vup_copies, wo_copies = [], []
    for ch in range(chunks):
        some = pl.ds(ch * qw * GROUP, qw * GROUP)
        vup_copies.append(pltpu.make_async_copy(vup_hbm.at[some], vup_v.at[some], vup_sem.at[ch]))
        vup_copies[-1].start()
    for ch in range(chunks):
        some = pl.ds(ch * qw * GROUP * VDIM, qw * GROUP * VDIM)
        wo_copies.append(pltpu.make_async_copy(wo_hbm.at[some], wo_v.at[some], wo_sem.at[ch]))
        wo_copies[-1].start()
    ffn_copies = [
        pltpu.make_async_copy(wg_hbm.at[0], wg_v, ffn_sem.at[0]),
        pltpu.make_async_copy(wu_hbm.at[0], wu_v, ffn_sem.at[1]),
        pltpu.make_async_copy(wd_hbm.at[0], wd_v, ffn_sem.at[2]),
    ]
    for copy in small_copies[1:] + ffn_copies:
        copy.start()

    sends = []

    def settle():
        for copy in sends:
            copy.wait_send()
        sends.clear()


    width = LANES // (2 * rl)
    stat_lane = lax.broadcasted_iota(jnp.int32, (heads, LANES), 1)
    place = c * positions + lax.broadcasted_iota(jnp.int32, (heads, positions), 1)
    stats = jnp.zeros((heads, LANES), F32)
    small_copies[0].wait()
    for r in range(rl):
        for copy in row_copies[r]:
            copy.wait()
        scores = lax.dot_general(
            q_v[r], kv_v[r], (((0,), (0,)), ((), ())), preferred_element_type=F32
        ) * SOFTMAX_SCALE
        valid = place < len_ref[r]
        masked = jnp.where(valid, scores, -1e30)
        top = jnp.max(masked, axis=1, keepdims=True)
        weights = jnp.where(valid, jnp.exp(masked - top), 0.0)
        total = jnp.sum(weights, axis=1, keepdims=True)
        numer = lax.dot_general(
            weights.astype(BF16), kv_v[r, :LATENT], (((1,), (1,)), ((), ())), preferred_element_type=F32
        )
        for j in range(nc):
            num_s[j, r] = numer[j * hpd : (j + 1) * hpd].astype(BF16)
        stats = jnp.where(stat_lane >= 2 * r * width, top, stats)
        stats = jnp.where(stat_lane >= (2 * r + 1) * width, total, stats)
    wide = rl * GROUP
    goal = lax.broadcasted_iota(jnp.int32, (rows * GROUP, ne * wide), 0)
    have = lax.broadcasted_iota(jnp.int32, (rows * GROUP, ne * wide), 1)
    target = (
        (have & (GROUP - 1)) * rows
        + lax.shift_right_logical(have, wide.bit_length() - 1) * rl
        + (lax.shift_right_logical(have, GROUP.bit_length() - 1) & (rl - 1))
    )
    shuffle = jnp.where(goal == target, 1.0, 0.0).astype(BF16)

    for j in range(nc):
        st_s[j] = stats[j * hpd : (j + 1) * hpd]
    pl.semaphore_wait(barrier, nc + ne - 2)
    for peer in ctx_peers:
        sends.append(remote(st_s.at[peer], st_r.at[c], st_ss.at[peer], st_rs.at[c], "ctx", peer))
        sends[-1].start()
        for r in range(rl):
            sends.append(
                remote(num_s.at[peer, r], num_r.at[c, r], num_ss.at[peer, r], num_rs.at[c, r], "ctx", peer)
            )
            sends[-1].start()

    for src in ctx_peers:
        remote(st_s.at[src], st_r.at[src], st_ss.at[src], st_rs.at[src], "ctx", src).wait_recv()
    for r in range(rl):
        for src in ctx_peers:
            remote(num_s.at[src, r], num_r.at[src, r], num_ss.at[src, r], num_rs.at[src, r], "ctx", src).wait_recv()
    all_stats = [st_s[c]] + [st_r[src] for src in ctx_peers]
    factors = []
    for r in range(rl):
        tops = [s[:, 2 * r * width : 2 * r * width + 1] for s in all_stats]
        totals = [s[:, (2 * r + 1) * width : (2 * r + 1) * width + 1] for s in all_stats]
        best = functools.reduce(jnp.maximum, tops)
        scale = [jnp.exp(t - best) for t in tops]
        whole = 1.0 / total_of([t * s for t, s in zip(totals, scale)])
        factors.append([s * whole for s in scale])
    row_of_group = lax.broadcasted_iota(jnp.int32, (wide, LATENT), 0) & (GROUP - 1)
    for ch in range(chunks):
        first = ch * qw * GROUP
        merged = []
        for r in range(rl):
            some = slice(first, first + qw * GROUP)
            parts = [num_s[c, r, some]] + [num_r[src, r, some] for src in ctx_peers]
            merged.append(
                total_of([p.astype(F32) * f[some] for p, f in zip(parts, factors[r])])
            )
        vup_copies[ch].wait()
        values = []
        for q in range(qw):
            left = jnp.concatenate([m[q * GROUP : (q + 1) * GROUP] for m in merged], axis=0)
            left = jnp.concatenate(
                [jnp.where(row_of_group == g, left, 0.0).astype(BF16) for g in range(GROUP)], axis=1
            )
            right = vup_v[first + q * GROUP : first + (q + 1) * GROUP].reshape(GROUP * LATENT, VDIM)
            values.append(jnp.dot(left, right, preferred_element_type=F32).astype(BF16))
        hv_r[ch, e] = jnp.concatenate(values, axis=1) if qw > 1 else values[0]
        for peer in ep_peers:
            sends.append(
                remote(hv_r.at[ch, e], hv_r.at[ch, e], hv_ss.at[ch, peer], hv_rs.at[ch, e], "ep", peer)
            )
            sends[-1].start()

    attn = None
    settle()
    for ch in range(chunks):
        for src in ep_peers:
            remote(hv_r.at[ch, src], hv_r.at[ch, src], hv_ss.at[ch, src], hv_rs.at[ch, src], "ep", src).wait_recv()
        came = hv_r[ch].reshape(ne * wide, qw * VDIM)
        sorted_values = jnp.dot(shuffle, came, preferred_element_type=F32).astype(BF16)
        left = jnp.concatenate(
            [
                sorted_values[g * rows : (g + 1) * rows, q * VDIM : (q + 1) * VDIM]
                for q in range(qw)
                for g in range(GROUP)
            ],
            axis=1,
        )
        wo_copies[ch].wait()
        depth = qw * GROUP * VDIM
        part = jnp.dot(left, wo_v[ch * depth : (ch + 1) * depth, :], preferred_element_type=F32)
        attn = part if attn is None else attn + part
    small_copies[1].wait()
    own_rows = lax.broadcasted_iota(jnp.int32, (rows, dl), 0) - c * ro
    spread = jnp.concatenate([res_ref[...].astype(F32)] * nc, axis=0)
    attn = attn + jnp.where((own_rows >= 0) & (own_rows < ro), spread, 0.0)
    ao_r[c] = attn.astype(BF16)
    for peer in ctx_peers:
        sends.append(remote(ao_r.at[c], ao_r.at[c], ao_ss.at[peer], ao_rs.at[c], "ctx", peer))
        sends[-1].start()
    settle()
    for src in ctx_peers:
        remote(ao_r.at[src], ao_r.at[src], ao_ss.at[src], ao_rs.at[src], "ctx", src).wait_recv()
        attn = attn + ao_r[src].astype(F32)

    hidden = attn.astype(BF16).astype(F32)
    for j in range(nc):
        hid_s[j] = hidden[j * ro : (j + 1) * ro]
    square = jnp.sum(hidden * hidden, axis=1, keepdims=True)
    high = square.astype(BF16).astype(F32)
    sq_lane = lax.broadcasted_iota(jnp.int32, (rows, LANES), 1)
    both = jnp.where(sq_lane < LANES // 2, high, square - high).astype(BF16)
    for j in range(rows // gr):
        sq_s[j] = both[j * gr : (j + 1) * gr]
    small_copies[2].wait()
    normed = (hidden * gain_ref[...].astype(F32).reshape(1, dl)).astype(BF16)
    ffn_copies[0].wait()
    gate = jnp.dot(normed, wg_v[...], preferred_element_type=F32)
    for peer in ep_peers:
        sends.append(
            remote(sq_s.at[peer // blocks], sq_r.at[e], sq_ss.at[peer], sq_rs.at[e], "ep", peer)
        )
        sends[-1].start()
    ffn_copies[1].wait()
    upper = jnp.dot(normed, wu_v[...], preferred_element_type=F32)
    for p in range(ne):
        some = slice(p // blocks * gr, (p // blocks + 1) * gr)
        cols = slice(p % blocks * LANES, (p % blocks + 1) * LANES)
        gu_s[p] = jnp.concatenate([gate[some, cols], upper[some, cols]], axis=1).astype(BF16)
    for peer in ep_peers:
        sends.append(remote(gu_s.at[peer], gu_r.at[e], gu_ss.at[peer], gu_rs.at[e], "ep", peer))
        sends[-1].start()
    settle()
    squares = sq_s[e // blocks].astype(F32)
    sums = gu_s[e].astype(F32)
    for src in ep_peers:
        remote(sq_s.at[0], sq_r.at[src], sq_ss.at[src], sq_rs.at[src], "ep", src).wait_recv()
        squares = squares + sq_r[src].astype(F32)
    for src in ep_peers:
        remote(gu_s.at[src], gu_r.at[src], gu_ss.at[src], gu_rs.at[src], "ep", src).wait_recv()
        sums = sums + gu_r[src].astype(F32)
    square = squares[:, :1] + squares[:, LANES // 2 : LANES // 2 + 1]
    inv_rms = lax.rsqrt(square / (dl * ne) + EPSILON)
    gate = inv_rms * sums[:, :LANES]
    upper = inv_rms * sums[:, LANES:]
    eh_r[e] = (gate / (1.0 + jnp.exp(-gate)) * upper).astype(BF16)
    for peer in ep_peers:
        sends.append(remote(eh_r.at[e], eh_r.at[e], eh_ss.at[peer], eh_rs.at[e], "ep", peer))
        sends[-1].start()
    settle()
    small_copies[3].wait()
    small_copies[4].wait()
    route = jnp.sum(jnp.where(ids_ref[...] == c, rw_ref[...], 0.0), axis=0, keepdims=True)
    diagonal = lax.broadcasted_iota(jnp.int32, (rows, rows), 0) == lax.broadcasted_iota(jnp.int32, (rows, rows), 1)
    route = jnp.sum(jnp.where(diagonal, route, 0.0), axis=1, keepdims=True)
    ffn_copies[2].wait()
    for src in ep_peers:
        remote(eh_r.at[src], eh_r.at[src], eh_ss.at[src], eh_rs.at[src], "ep", src).wait_recv()

    left = [
        jnp.concatenate([eh_r[j * blocks + b] for b in range(blocks)], axis=1) for j in range(rows // gr)
    ]
    left = jnp.concatenate(left, axis=0) if len(left) > 1 else left[0]
    expert = route * jnp.dot(left, wd_v[...], preferred_element_type=F32)
    for j in range(nc):
        mo_s[j] = expert[j * ro : (j + 1) * ro]
    for peer in ctx_peers:
        sends.append(remote(mo_s.at[peer], mo_r.at[c], mo_ss.at[peer], mo_rs.at[c], "ctx", peer))
        sends[-1].start()
    settle()
    result = hid_s[c] + mo_s[c]
    for src in ctx_peers:
        remote(mo_s.at[src], mo_r.at[src], mo_ss.at[src], mo_rs.at[src], "ctx", src).wait_recv()
        result = result + mo_r[src]
    out_ref[...] = result.astype(BF16)


def local(
    nc, ne, queries, latent_cache, lengths, value_up, out_proj, residual, norm_gain,
    expert_ids, route_weight, gate_proj, up_proj, down_proj,
):
    rl, heads, width = queries.shape
    positions = latent_cache.shape[1]
    hpd = value_up.shape[0]
    ro, dl = residual.shape
    rows = expert_ids.shape[0]
    ffw = gate_proj.shape[2]
    blocks = ffw // LANES
    gr = rows * blocks // ne
    nq = hpd // GROUP
    chunks = 2 if nq % 2 == 0 else 1
    qw = nq // chunks
    wide = rl * GROUP
    vm = pltpu.VMEM
    dma = pltpu.SemaphoreType.DMA
    scratch = [
        vm((rl, width, heads), BF16),
        vm((rl, width, positions), BF16),
        vm(value_up.shape, BF16),
        vm(out_proj.shape, BF16),
        vm(gate_proj.shape[1:], BF16),
        vm(up_proj.shape[1:], BF16),
        vm(down_proj.shape[1:], BF16),
        pltpu.SMEM((rl,), jnp.int32),
        vm((ro, dl), BF16),
        vm((dl,), BF16),
        vm((expert_ids.shape[1], rows), jnp.int32),
        vm((expert_ids.shape[1], rows), F32),
        vm((nc, rl, hpd, LATENT), BF16),
        vm((nc, rl, hpd, LATENT), BF16),
        vm((nc, hpd, LANES), F32),
        vm((nc, hpd, LANES), F32),
        vm((chunks, ne, wide, qw * VDIM), BF16),
        vm((nc, rows, dl), BF16),
        vm((nc, ro, dl), F32),
        vm((rows // gr, gr, LANES), BF16),
        vm((ne, gr, LANES), BF16),
        vm((ne, gr, 2 * LANES), BF16),
        vm((ne, gr, 2 * LANES), BF16),
        vm((ne, gr, LANES), BF16),
        vm((nc, ro, dl), F32),
        vm((nc, ro, dl), F32),
        dma((rl, 2)),
        dma((chunks,)),
        dma((chunks,)),
        dma((3,)),
        dma((5,)),
    ]
    for shape in ((nc, rl), (nc,), (chunks, ne), (nc,), (ne,), (ne,), (ne,), (nc,)):
        scratch += [dma(shape), dma(shape)]
    weights = value_up.size + out_proj.size + gate_proj.size + up_proj.size + down_proj.size
    return pl.pallas_call(
        functools.partial(kernel, nc, ne, chunks),
        out_shape=jax.ShapeDtypeStruct((ro, dl), BF16),
        in_specs=[pl.BlockSpec(memory_space=pl.ANY)] * 12,
        out_specs=pl.BlockSpec(memory_space=pltpu.VMEM),
        scratch_shapes=scratch,
        compiler_params=pltpu.CompilerParams(
            collective_id=0, has_side_effects=True, vmem_limit_bytes=63 * 2**20
        ),
        cost_estimate=pl.CostEstimate(
            flops=2 * rows * weights, bytes_accessed=2 * weights, transcendentals=rl * heads * positions
        ),
        name="decode_step",
    )(
        queries.transpose(0, 2, 1), latent_cache.transpose(0, 2, 1), lengths, value_up, out_proj, residual,
        norm_gain, expert_ids.T, route_weight.T, gate_proj, up_proj, down_proj,
    )


def solution(mesh):
    placed = (
        P("ep", None, None),
        P("ep", "ctx", None),
        P("ep"),
        P("ctx", None, None),
        P("ctx", "ep"),
        P("ctx", "ep"),
        P("ep"),
        P(),
        P(),
        P("ctx", "ep", None),
        P("ctx", "ep", None),
        P("ctx", None, "ep"),
    )
    step = functools.partial(local, mesh.shape["ctx"], mesh.shape["ep"])
    return jax.shard_map(step, mesh=mesh, in_specs=placed, out_specs=P("ctx", "ep"), check_vma=False)
```

```python
import functools

import jax
import jax.numpy as jnp
from jax import lax
from jax.experimental import pallas as pl
from jax.experimental.pallas import tpu as pltpu
from jax.sharding import PartitionSpec as P

LATENT = 512
VDIM = 128
LANES = 128
GROUP = 8
SOFTMAX_SCALE = 192.0 ** (-0.5)
EPSILON = 1e-06
MESH = pl.DeviceIdType.MESH
BF16 = jnp.bfloat16
F32 = jnp.float32


def remote(src, dst, send_sem, recv_sem, axis, peer):
    return pltpu.make_async_remote_copy(
        src_ref=src,
        dst_ref=dst,
        send_sem=send_sem,
        recv_sem=recv_sem,
        device_id={axis: peer},
        device_id_type=MESH,
    )


def flipped(index, bits):
    result, bit = index, 1
    while bit <= bits:
        if bits & bit:
            result = result + bit - 2 * bit * lax.rem(lax.div(index, bit), 2)
        bit *= 2
    return result


def bf16_terms(value, count):
    terms = []
    for _ in range(count):
        terms.append(value.astype(BF16).astype(F32))
        value = value - terms[-1]
    return terms


def total_of(parts):
    result = parts[0]
    for part in parts[1:]:
        result = result + part
    return result


def kernel(
    nc, ne, chunks,
    q_hbm, kv_hbm, len_hbm, vup_hbm, wo_hbm, res_hbm, gain_hbm, ids_hbm, rw_hbm, wg_hbm, wu_hbm, wd_hbm,
    out_ref,
    q_v, kv_v, vup_v, wo_v, wg_v, wu_v, wd_v, len_ref, res_ref, gain_ref, ids_ref, rw_ref,
    num_s, num_r, st_s, st_r, hv_r, ao_r, hid_s, sq_s, sq_r, gu_s, gu_r, eh_r, mo_s, mo_r,
    row_sem, vup_sem, wo_sem, ffn_sem, small_sem,
    num_ss, num_rs, st_ss, st_rs, hv_ss, hv_rs, ao_ss, ao_rs,
    sq_ss, sq_rs, gu_ss, gu_rs, eh_ss, eh_rs, mo_ss, mo_rs,
):
    c = lax.axis_index("ctx")
    e = lax.axis_index("ep")
    rl, _, heads = q_v.shape
    positions = kv_v.shape[2]
    hpd = vup_v.shape[0]
    hc = hpd // chunks
    qw = hc // GROUP
    rows = ao_r.shape[1]
    dl = ao_r.shape[2]
    ro = rows // nc
    ffw = wg_v.shape[1]
    blocks = ffw // LANES
    gr = gu_s.shape[1]

    ctx_peers = [flipped(c, bits) for bits in reversed(range(1, nc))]
    ep_peers = [flipped(e, bits) for bits in reversed(range(1, ne))]

    small_copies = [
        pltpu.make_async_copy(src, dst, small_sem.at[k])
        for k, (src, dst) in enumerate(
            ((len_hbm, len_ref), (res_hbm, res_ref), (gain_hbm, gain_ref), (ids_hbm, ids_ref), (rw_hbm, rw_ref))
        )
    ]
    small_copies[0].start()
    row_copies = []
    for r in range(rl):
        pair = (
            pltpu.make_async_copy(q_hbm.at[r], q_v.at[r], row_sem.at[r, 0]),
            pltpu.make_async_copy(kv_hbm.at[r], kv_v.at[r], row_sem.at[r, 1]),
        )
        row_copies.append(pair)
        for copy in pair:
            copy.start()

    barrier = pltpu.get_barrier_semaphore()
    for peer in ctx_peers:
        pl.semaphore_signal(barrier, inc=1, device_id={"ctx": peer}, device_id_type=MESH)
    for peer in ep_peers:
        pl.semaphore_signal(barrier, inc=1, device_id={"ep": peer}, device_id_type=MESH)

    vup_copies, wo_copies = [], []
    for ch in range(chunks):
        some = pl.ds(ch * qw * GROUP, qw * GROUP)
        vup_copies.append(pltpu.make_async_copy(vup_hbm.at[some], vup_v.at[some], vup_sem.at[ch]))
        vup_copies[-1].start()
    for ch in range(chunks):
        some = pl.ds(ch * qw * GROUP * VDIM, qw * GROUP * VDIM)
        wo_copies.append(pltpu.make_async_copy(wo_hbm.at[some], wo_v.at[some], wo_sem.at[ch]))
        wo_copies[-1].start()
    ffn_copies = [
        pltpu.make_async_copy(wg_hbm.at[0], wg_v, ffn_sem.at[0]),
        pltpu.make_async_copy(wu_hbm.at[0], wu_v, ffn_sem.at[1]),
        pltpu.make_async_copy(wd_hbm.at[0], wd_v, ffn_sem.at[2]),
    ]
    for copy in small_copies[1:] + ffn_copies:
        copy.start()

    sends = []

    def settle():
        for copy in sends:
            copy.wait_send()
        sends.clear()


    terms = 5
    width = LANES // (terms * rl)
    stat_lane = lax.broadcasted_iota(jnp.int32, (heads, LANES), 1)
    place = c * positions + lax.broadcasted_iota(jnp.int32, (heads, positions), 1)
    stats = jnp.zeros((heads, LANES), F32)
    small_copies[0].wait()
    for r in range(rl):
        for copy in row_copies[r]:
            copy.wait()
        scores = lax.dot_general(
            q_v[r], kv_v[r], (((0,), (0,)), ((), ())), preferred_element_type=F32
        ) * SOFTMAX_SCALE
        valid = place < len_ref[r]
        masked = jnp.where(valid, scores, -1e30)
        top = jnp.max(masked, axis=1, keepdims=True)
        weights = jnp.where(valid, jnp.exp(masked - top), 0.0)
        total = jnp.sum(weights, axis=1, keepdims=True)
        numer = lax.dot_general(
            weights.astype(BF16), kv_v[r, :LATENT], (((1,), (1,)), ((), ())), preferred_element_type=F32
        )
        for j in range(nc):
            for ch in range(chunks):
                num_s[j, ch, r] = numer[j * hpd + ch * hc : j * hpd + (ch + 1) * hc].astype(BF16)
        for k, term in enumerate(bf16_terms(top, 3) + bf16_terms(total, 2)):
            stats = jnp.where(stat_lane >= (terms * r + k) * width, term, stats)
    wide = rl * GROUP
    goal = lax.broadcasted_iota(jnp.int32, (rows * GROUP, ne * wide), 0)
    have = lax.broadcasted_iota(jnp.int32, (rows * GROUP, ne * wide), 1)
    target = (
        (have & (GROUP - 1)) * rows
        + lax.shift_right_logical(have, wide.bit_length() - 1) * rl
        + (lax.shift_right_logical(have, GROUP.bit_length() - 1) & (rl - 1))
    )
    shuffle = jnp.where(goal == target, 1.0, 0.0).astype(BF16)

    for j in range(nc):
        st_s[j] = stats[j * hpd : (j + 1) * hpd].astype(BF16)
    pl.semaphore_wait(barrier, nc + ne - 2)
    for peer in ctx_peers:
        sends.append(remote(st_s.at[peer], st_r.at[c], st_ss.at[peer], st_rs.at[c], "ctx", peer))
        sends[-1].start()
    for ch in range(chunks):
        for peer in ctx_peers:
            sends.append(
                remote(num_s.at[peer, ch], num_r.at[c, ch], num_ss.at[peer, ch], num_rs.at[c, ch], "ctx", peer)
            )
            sends[-1].start()

    for src in ctx_peers:
        remote(st_s.at[src], st_r.at[src], st_ss.at[src], st_rs.at[src], "ctx", src).wait_recv()
    all_stats = [st_s[c].astype(F32)] + [st_r[src].astype(F32) for src in ctx_peers]
    factors = []
    for r in range(rl):
        lanes = [[s[:, n * width : n * width + 1] for n in range(terms * r, terms * (r + 1))] for s in all_stats]
        tops = [total_of(t[:3]) for t in lanes]
        totals = [total_of(t[3:]) for t in lanes]
        best = functools.reduce(jnp.maximum, tops)
        scale = [jnp.exp(t - best) for t in tops]
        whole = 1.0 / total_of([t * s for t, s in zip(totals, scale)])
        factors.append([s * whole for s in scale])
    row_of_group = lax.broadcasted_iota(jnp.int32, (wide, LATENT), 0) & (GROUP - 1)
    for ch in range(chunks):
        first = ch * hc
        for src in ctx_peers:
            remote(
                num_s.at[src, ch], num_r.at[src, ch], num_ss.at[src, ch], num_rs.at[src, ch], "ctx", src
            ).wait_recv()
        merged = []
        for r in range(rl):
            some = slice(first, first + hc)
            parts = [num_s[c, ch, r]] + [num_r[src, ch, r] for src in ctx_peers]
            merged.append(
                total_of([p.astype(F32) * f[some] for p, f in zip(parts, factors[r])])
            )
        vup_copies[ch].wait()
        values = []
        for q in range(qw):
            left = jnp.concatenate([m[q * GROUP : (q + 1) * GROUP] for m in merged], axis=0)
            left = jnp.concatenate(
                [jnp.where(row_of_group == g, left, 0.0).astype(BF16) for g in range(GROUP)], axis=1
            )
            right = vup_v[first + q * GROUP : first + (q + 1) * GROUP].reshape(GROUP * LATENT, VDIM)
            values.append(jnp.dot(left, right, preferred_element_type=F32).astype(BF16))
        hv_r[ch, e] = jnp.concatenate(values, axis=1) if qw > 1 else values[0]
        for peer in ep_peers:
            sends.append(
                remote(hv_r.at[ch, e], hv_r.at[ch, e], hv_ss.at[ch, peer], hv_rs.at[ch, e], "ep", peer)
            )
            sends[-1].start()

    attn = None
    settle()
    for ch in range(chunks):
        for src in ep_peers:
            remote(hv_r.at[ch, src], hv_r.at[ch, src], hv_ss.at[ch, src], hv_rs.at[ch, src], "ep", src).wait_recv()
        came = hv_r[ch].reshape(ne * wide, qw * VDIM)
        sorted_values = jnp.dot(shuffle, came, preferred_element_type=F32).astype(BF16)
        left = jnp.concatenate(
            [
                sorted_values[g * rows : (g + 1) * rows, q * VDIM : (q + 1) * VDIM]
                for q in range(qw)
                for g in range(GROUP)
            ],
            axis=1,
        )
        wo_copies[ch].wait()
        depth = qw * GROUP * VDIM
        part = jnp.dot(left, wo_v[ch * depth : (ch + 1) * depth, :], preferred_element_type=F32)
        attn = part if attn is None else attn + part
    small_copies[1].wait()
    own_rows = lax.broadcasted_iota(jnp.int32, (rows, dl), 0) - c * ro
    spread = jnp.concatenate([res_ref[...].astype(F32)] * nc, axis=0)
    attn = attn + jnp.where((own_rows >= 0) & (own_rows < ro), spread, 0.0)
    ao_r[c] = attn.astype(BF16)
    for peer in ctx_peers:
        sends.append(remote(ao_r.at[c], ao_r.at[c], ao_ss.at[peer], ao_rs.at[c], "ctx", peer))
        sends[-1].start()
    settle()
    for src in ctx_peers:
        remote(ao_r.at[src], ao_r.at[src], ao_ss.at[src], ao_rs.at[src], "ctx", src).wait_recv()
        attn = attn + ao_r[src].astype(F32)

    hidden = attn.astype(BF16).astype(F32)
    for j in range(nc):
        hid_s[j] = hidden[j * ro : (j + 1) * ro]
    square = jnp.sum(hidden * hidden, axis=1, keepdims=True)
    high = square.astype(BF16).astype(F32)
    sq_lane = lax.broadcasted_iota(jnp.int32, (rows, LANES), 1)
    both = jnp.where(sq_lane < LANES // 2, high, square - high).astype(BF16)
    for j in range(rows // gr):
        sq_s[j] = both[j * gr : (j + 1) * gr]
    small_copies[2].wait()
    normed = (hidden * gain_ref[...].astype(F32).reshape(1, dl)).astype(BF16)
    ffn_copies[0].wait()
    gate = jnp.dot(normed, wg_v[...], preferred_element_type=F32)
    for peer in ep_peers:
        sends.append(
            remote(sq_s.at[peer // blocks], sq_r.at[e], sq_ss.at[peer], sq_rs.at[e], "ep", peer)
        )
        sends[-1].start()
    ffn_copies[1].wait()
    upper = jnp.dot(normed, wu_v[...], preferred_element_type=F32)
    for p in range(ne):
        some = slice(p // blocks * gr, (p // blocks + 1) * gr)
        cols = slice(p % blocks * LANES, (p % blocks + 1) * LANES)
        gu_s[p] = jnp.concatenate([gate[some, cols], upper[some, cols]], axis=1).astype(BF16)
    for peer in ep_peers:
        sends.append(remote(gu_s.at[peer], gu_r.at[e], gu_ss.at[peer], gu_rs.at[e], "ep", peer))
        sends[-1].start()
    settle()
    squares = sq_s[e // blocks].astype(F32)
    sums = gu_s[e].astype(F32)
    for src in ep_peers:
        remote(sq_s.at[0], sq_r.at[src], sq_ss.at[src], sq_rs.at[src], "ep", src).wait_recv()
        squares = squares + sq_r[src].astype(F32)
    for src in ep_peers:
        remote(gu_s.at[src], gu_r.at[src], gu_ss.at[src], gu_rs.at[src], "ep", src).wait_recv()
        sums = sums + gu_r[src].astype(F32)
    square = squares[:, :1] + squares[:, LANES // 2 : LANES // 2 + 1]
    inv_rms = lax.rsqrt(square / (dl * ne) + EPSILON)
    gate = inv_rms * sums[:, :LANES]
    upper = inv_rms * sums[:, LANES:]
    eh_r[e] = (gate / (1.0 + jnp.exp(-gate)) * upper).astype(BF16)
    for peer in ep_peers:
        sends.append(remote(eh_r.at[e], eh_r.at[e], eh_ss.at[peer], eh_rs.at[e], "ep", peer))
        sends[-1].start()
    settle()
    small_copies[3].wait()
    small_copies[4].wait()
    route = jnp.sum(jnp.where(ids_ref[...] == c, rw_ref[...], 0.0), axis=0, keepdims=True)
    diagonal = lax.broadcasted_iota(jnp.int32, (rows, rows), 0) == lax.broadcasted_iota(jnp.int32, (rows, rows), 1)
    route = jnp.sum(jnp.where(diagonal, route, 0.0), axis=1, keepdims=True)
    ffn_copies[2].wait()
    for src in ep_peers:
        remote(eh_r.at[src], eh_r.at[src], eh_ss.at[src], eh_rs.at[src], "ep", src).wait_recv()

    left = [
        jnp.concatenate([eh_r[j * blocks + b] for b in range(blocks)], axis=1) for j in range(rows // gr)
    ]
    left = jnp.concatenate(left, axis=0) if len(left) > 1 else left[0]
    expert = route * jnp.dot(left, wd_v[...], preferred_element_type=F32)
    for j in range(nc):
        mo_s[j] = expert[j * ro : (j + 1) * ro].astype(BF16)
    for peer in ctx_peers:
        sends.append(remote(mo_s.at[peer], mo_r.at[c], mo_ss.at[peer], mo_rs.at[c], "ctx", peer))
        sends[-1].start()
    settle()
    result = hid_s[c] + mo_s[c].astype(F32)
    for src in ctx_peers:
        remote(mo_s.at[src], mo_r.at[src], mo_ss.at[src], mo_rs.at[src], "ctx", src).wait_recv()
        result = result + mo_r[src].astype(F32)
    out_ref[...] = result.astype(BF16)


def local(
    nc, ne, queries, latent_cache, lengths, value_up, out_proj, residual, norm_gain,
    expert_ids, route_weight, gate_proj, up_proj, down_proj,
):
    rl, heads, width = queries.shape
    positions = latent_cache.shape[1]
    hpd = value_up.shape[0]
    ro, dl = residual.shape
    rows = expert_ids.shape[0]
    ffw = gate_proj.shape[2]
    blocks = ffw // LANES
    gr = rows * blocks // ne
    nq = hpd // GROUP
    chunks = 2 if nq % 2 == 0 else 1
    qw = nq // chunks
    wide = rl * GROUP
    vm = pltpu.VMEM
    dma = pltpu.SemaphoreType.DMA
    scratch = [
        vm((rl, width, heads), BF16),
        vm((rl, width, positions), BF16),
        vm(value_up.shape, BF16),
        vm(out_proj.shape, BF16),
        vm(gate_proj.shape[1:], BF16),
        vm(up_proj.shape[1:], BF16),
        vm(down_proj.shape[1:], BF16),
        pltpu.SMEM((rl,), jnp.int32),
        vm((ro, dl), BF16),
        vm((dl,), BF16),
        vm((expert_ids.shape[1], rows), jnp.int32),
        vm((expert_ids.shape[1], rows), F32),
        vm((nc, chunks, rl, hpd // chunks, LATENT), BF16),
        vm((nc, chunks, rl, hpd // chunks, LATENT), BF16),
        vm((nc, hpd, LANES), BF16),
        vm((nc, hpd, LANES), BF16),
        vm((chunks, ne, wide, qw * VDIM), BF16),
        vm((nc, rows, dl), BF16),
        vm((nc, ro, dl), F32),
        vm((rows // gr, gr, LANES), BF16),
        vm((ne, gr, LANES), BF16),
        vm((ne, gr, 2 * LANES), BF16),
        vm((ne, gr, 2 * LANES), BF16),
        vm((ne, gr, LANES), BF16),
        vm((nc, ro, dl), BF16),
        vm((nc, ro, dl), BF16),
        dma((rl, 2)),
        dma((chunks,)),
        dma((chunks,)),
        dma((3,)),
        dma((5,)),
    ]
    for shape in ((nc, chunks), (nc,), (chunks, ne), (nc,), (ne,), (ne,), (ne,), (nc,)):
        scratch += [dma(shape), dma(shape)]
    weights = value_up.size + out_proj.size + gate_proj.size + up_proj.size + down_proj.size
    return pl.pallas_call(
        functools.partial(kernel, nc, ne, chunks),
        out_shape=jax.ShapeDtypeStruct((ro, dl), BF16),
        in_specs=[pl.BlockSpec(memory_space=pl.ANY)] * 12,
        out_specs=pl.BlockSpec(memory_space=pltpu.VMEM),
        scratch_shapes=scratch,
        compiler_params=pltpu.CompilerParams(
            collective_id=0, has_side_effects=True, vmem_limit_bytes=63 * 2**20
        ),
        cost_estimate=pl.CostEstimate(
            flops=2 * rows * weights, bytes_accessed=2 * weights, transcendentals=rl * heads * positions
        ),
        name="decode_step",
    )(
        queries.transpose(0, 2, 1), latent_cache.transpose(0, 2, 1), lengths, value_up, out_proj, residual,
        norm_gain, expert_ids.T, route_weight.T, gate_proj, up_proj, down_proj,
    )


def solution(mesh):
    placed = (
        P("ep", None, None),
        P("ep", "ctx", None),
        P("ep"),
        P("ctx", None, None),
        P("ctx", "ep"),
        P("ctx", "ep"),
        P("ep"),
        P(),
        P(),
        P("ctx", "ep", None),
        P("ctx", "ep", None),
        P("ctx", None, "ep"),
    )
    step = functools.partial(local, mesh.shape["ctx"], mesh.shape["ep"])
    return jax.shard_map(step, mesh=mesh, in_specs=placed, out_specs=P("ctx", "ep"), check_vma=False)
```

```python
import functools

import jax
import jax.numpy as jnp
from jax import lax
from jax.experimental import pallas as pl
from jax.experimental.pallas import tpu as pltpu
from jax.sharding import PartitionSpec as P

LATENT = 512
VDIM = 128
LANES = 128
GROUP = 8
SOFTMAX_SCALE = 192.0 ** (-0.5)
EPSILON = 1e-06
MESH = pl.DeviceIdType.MESH
BF16 = jnp.bfloat16
F32 = jnp.float32


def remote(src, dst, send_sem, recv_sem, axis, peer):
    return pltpu.make_async_remote_copy(
        src_ref=src,
        dst_ref=dst,
        send_sem=send_sem,
        recv_sem=recv_sem,
        device_id={axis: peer},
        device_id_type=MESH,
    )


def flipped(index, bits):
    result, bit = index, 1
    while bit <= bits:
        if bits & bit:
            result = result + bit - 2 * bit * lax.rem(lax.div(index, bit), 2)
        bit *= 2
    return result


def bf16_terms(value, count):
    terms = []
    for _ in range(count):
        terms.append(value.astype(BF16).astype(F32))
        value = value - terms[-1]
    return terms


def total_of(parts):
    result = parts[0]
    for part in parts[1:]:
        result = result + part
    return result


def kernel(
    nc, ne, chunks,
    q_hbm, kv_hbm, len_hbm, vup_hbm, wo_hbm, res_hbm, gain_hbm, ids_hbm, rw_hbm, wg_hbm, wu_hbm, wd_hbm,
    out_ref,
    q_v, kv_v, vup_v, wo_v, wg_v, wu_v, wd_v, len_ref, res_ref, gain_ref, ids_ref, rw_ref,
    num_s, num_r, st_s, st_r, hv_r, ao_a, ao_b, hid_s, sq_s, sq_r, gu_s, gu_r, eh_r, mo_s, mo_r,
    row_sem, vup_sem, wo_sem, ffn_sem, small_sem,
    num_ss, num_rs, st_ss, st_rs, hv_ss, hv_rs, ao_ss, ao_rs,
    sq_ss, sq_rs, gu_ss, gu_rs, eh_ss, eh_rs, mo_ss, mo_rs,
):
    c = lax.axis_index("ctx")
    e = lax.axis_index("ep")
    rl, _, heads = q_v.shape
    positions = kv_v.shape[2]
    hpd = vup_v.shape[0]
    hc = hpd // chunks
    qw = hc // GROUP
    rows = ids_ref.shape[1]
    dl = wo_v.shape[1]
    ao_r = (ao_a, ao_b)
    cut = ao_a.shape[2]
    cuts = (slice(0, cut), slice(cut, dl))
    ro = rows // nc
    ffw = wg_v.shape[1]
    blocks = ffw // LANES
    gr = gu_s.shape[1]

    ctx_peers = [flipped(c, bits) for bits in reversed(range(1, nc))]
    ep_peers = [flipped(e, bits) for bits in reversed(range(1, ne))]

    small_copies = [
        pltpu.make_async_copy(src, dst, small_sem.at[k])
        for k, (src, dst) in enumerate(
            ((len_hbm, len_ref), (res_hbm, res_ref), (gain_hbm, gain_ref), (ids_hbm, ids_ref), (rw_hbm, rw_ref))
        )
    ]
    small_copies[0].start()
    row_copies = []
    for r in range(rl):
        pair = (
            pltpu.make_async_copy(q_hbm.at[r], q_v.at[r], row_sem.at[r, 0]),
            pltpu.make_async_copy(kv_hbm.at[r], kv_v.at[r], row_sem.at[r, 1]),
        )
        row_copies.append(pair)
        for copy in pair:
            copy.start()

    barrier = pltpu.get_barrier_semaphore()
    for peer in ctx_peers:
        pl.semaphore_signal(barrier, inc=1, device_id={"ctx": peer}, device_id_type=MESH)
    for peer in ep_peers:
        pl.semaphore_signal(barrier, inc=1, device_id={"ep": peer}, device_id_type=MESH)

    vup_copies, wo_copies = [], []
    for ch in range(chunks):
        some = pl.ds(ch * qw * GROUP, qw * GROUP)
        vup_copies.append(pltpu.make_async_copy(vup_hbm.at[some], vup_v.at[some], vup_sem.at[ch]))
        vup_copies[-1].start()
    for ch in range(chunks):
        some = pl.ds(ch * qw * GROUP * VDIM, qw * GROUP * VDIM)
        wo_copies.append(pltpu.make_async_copy(wo_hbm.at[some], wo_v.at[some], wo_sem.at[ch]))
        wo_copies[-1].start()
    ffn_copies = [
        pltpu.make_async_copy(wg_hbm.at[0], wg_v, ffn_sem.at[0]),
        pltpu.make_async_copy(wu_hbm.at[0], wu_v, ffn_sem.at[1]),
        pltpu.make_async_copy(wd_hbm.at[0], wd_v, ffn_sem.at[2]),
    ]
    for copy in small_copies[1:] + ffn_copies:
        copy.start()

    sends = []

    def settle():
        for copy in sends:
            copy.wait_send()
        sends.clear()


    terms = 5
    width = LANES // (terms * rl)
    stat_lane = lax.broadcasted_iota(jnp.int32, (heads, LANES), 1)
    place = c * positions + lax.broadcasted_iota(jnp.int32, (heads, positions), 1)
    stats = jnp.zeros((heads, LANES), F32)
    small_copies[0].wait()
    for r in range(rl):
        for copy in row_copies[r]:
            copy.wait()
        scores = lax.dot_general(
            q_v[r], kv_v[r], (((0,), (0,)), ((), ())), preferred_element_type=F32
        ) * SOFTMAX_SCALE
        valid = place < len_ref[r]
        masked = jnp.where(valid, scores, -1e30)
        top = jnp.max(masked, axis=1, keepdims=True)
        weights = jnp.where(valid, jnp.exp(masked - top), 0.0)
        total = jnp.sum(weights, axis=1, keepdims=True)
        numer = lax.dot_general(
            weights.astype(BF16), kv_v[r, :LATENT], (((1,), (1,)), ((), ())), preferred_element_type=F32
        )
        for j in range(nc):
            for ch in range(chunks):
                num_s[j, ch, r] = numer[j * hpd + ch * hc : j * hpd + (ch + 1) * hc].astype(BF16)
        for k, term in enumerate(bf16_terms(top, 3) + bf16_terms(total, 2)):
            stats = jnp.where(stat_lane >= (terms * r + k) * width, term, stats)
    wide = rl * GROUP
    goal = lax.broadcasted_iota(jnp.int32, (rows * GROUP, ne * wide), 0)
    have = lax.broadcasted_iota(jnp.int32, (rows * GROUP, ne * wide), 1)
    target = (
        (have & (GROUP - 1)) * rows
        + lax.shift_right_logical(have, wide.bit_length() - 1) * rl
        + (lax.shift_right_logical(have, GROUP.bit_length() - 1) & (rl - 1))
    )
    shuffle = jnp.where(goal == target, 1.0, 0.0).astype(BF16)

    for j in range(nc):
        st_s[j] = stats[j * hpd : (j + 1) * hpd].astype(BF16)
    pl.semaphore_wait(barrier, nc + ne - 2)
    for peer in ctx_peers:
        sends.append(remote(st_s.at[peer], st_r.at[c], st_ss.at[peer], st_rs.at[c], "ctx", peer))
        sends[-1].start()
    for ch in range(chunks):
        for peer in ctx_peers:
            sends.append(
                remote(num_s.at[peer, ch], num_r.at[c, ch], num_ss.at[peer, ch], num_rs.at[c, ch], "ctx", peer)
            )
            sends[-1].start()

    for src in ctx_peers:
        remote(st_s.at[src], st_r.at[src], st_ss.at[src], st_rs.at[src], "ctx", src).wait_recv()
    all_stats = [st_s[c].astype(F32)] + [st_r[src].astype(F32) for src in ctx_peers]
    factors = []
    for r in range(rl):
        lanes = [[s[:, n * width : n * width + 1] for n in range(terms * r, terms * (r + 1))] for s in all_stats]
        tops = [total_of(t[:3]) for t in lanes]
        totals = [total_of(t[3:]) for t in lanes]
        best = functools.reduce(jnp.maximum, tops)
        scale = [jnp.exp(t - best) for t in tops]
        whole = 1.0 / total_of([t * s for t, s in zip(totals, scale)])
        factors.append([s * whole for s in scale])
    row_of_group = lax.broadcasted_iota(jnp.int32, (wide, LATENT), 0) & (GROUP - 1)
    for ch in range(chunks):
        first = ch * hc
        for src in ctx_peers:
            remote(
                num_s.at[src, ch], num_r.at[src, ch], num_ss.at[src, ch], num_rs.at[src, ch], "ctx", src
            ).wait_recv()
        merged = []
        for r in range(rl):
            some = slice(first, first + hc)
            parts = [num_s[c, ch, r]] + [num_r[src, ch, r] for src in ctx_peers]
            merged.append(
                total_of([p.astype(F32) * f[some] for p, f in zip(parts, factors[r])])
            )
        vup_copies[ch].wait()
        values = []
        for q in range(qw):
            left = jnp.concatenate([m[q * GROUP : (q + 1) * GROUP] for m in merged], axis=0)
            left = jnp.concatenate(
                [jnp.where(row_of_group == g, left, 0.0).astype(BF16) for g in range(GROUP)], axis=1
            )
            right = vup_v[first + q * GROUP : first + (q + 1) * GROUP].reshape(GROUP * LATENT, VDIM)
            values.append(jnp.dot(left, right, preferred_element_type=F32).astype(BF16))
        hv_r[ch, e] = jnp.concatenate(values, axis=1) if qw > 1 else values[0]
        for peer in ep_peers:
            sends.append(
                remote(hv_r.at[ch, e], hv_r.at[ch, e], hv_ss.at[ch, peer], hv_rs.at[ch, e], "ep", peer)
            )
            sends[-1].start()

    settle()
    lefts = []
    for ch in range(chunks):
        for src in ep_peers:
            remote(hv_r.at[ch, src], hv_r.at[ch, src], hv_ss.at[ch, src], hv_rs.at[ch, src], "ep", src).wait_recv()
        came = hv_r[ch].reshape(ne * wide, qw * VDIM)
        sorted_values = jnp.dot(shuffle, came, preferred_element_type=F32).astype(BF16)
        lefts.append(
            jnp.concatenate(
                [
                    sorted_values[g * rows : (g + 1) * rows, q * VDIM : (q + 1) * VDIM]
                    for q in range(qw)
                    for g in range(GROUP)
                ],
                axis=1,
            )
        )
        wo_copies[ch].wait()
    small_copies[1].wait()
    depth = hc * VDIM
    own_rows = lax.broadcasted_iota(jnp.int32, (rows, dl), 0) - c * ro
    spread = jnp.concatenate([res_ref[...].astype(F32)] * nc, axis=0)
    spread = jnp.where((own_rows >= 0) & (own_rows < ro), spread, 0.0)
    parts = []
    for k, cols in enumerate(cuts):
        parts.append(
            spread[:, cols]
            + total_of(
                [
                    jnp.dot(left, wo_v[ch * depth : (ch + 1) * depth, cols], preferred_element_type=F32)
                    for ch, left in enumerate(lefts)
                ]
            )
        )
        ao_r[k][c] = parts[-1].astype(BF16)
        for peer in ctx_peers:
            sends.append(
                remote(ao_r[k].at[c], ao_r[k].at[c], ao_ss.at[k, peer], ao_rs.at[k, c], "ctx", peer)
            )
            sends[-1].start()
    settle()
    for k in range(len(cuts)):
        for src in ctx_peers:
            remote(ao_r[k].at[src], ao_r[k].at[src], ao_ss.at[k, src], ao_rs.at[k, src], "ctx", src).wait_recv()
            parts[k] = parts[k] + ao_r[k][src].astype(F32)
    attn = jnp.concatenate(parts, axis=1) if len(parts) > 1 else parts[0]

    hidden = attn.astype(BF16).astype(F32)
    for j in range(nc):
        hid_s[j] = hidden[j * ro : (j + 1) * ro]
    square = jnp.sum(hidden * hidden, axis=1, keepdims=True)
    high = square.astype(BF16).astype(F32)
    sq_lane = lax.broadcasted_iota(jnp.int32, (rows, LANES), 1)
    both = jnp.where(sq_lane < LANES // 2, high, square - high).astype(BF16)
    for j in range(rows // gr):
        sq_s[j] = both[j * gr : (j + 1) * gr]
    small_copies[2].wait()
    normed = (hidden * gain_ref[...].astype(F32).reshape(1, dl)).astype(BF16)
    ffn_copies[0].wait()
    gate = jnp.dot(normed, wg_v[...], preferred_element_type=F32)
    for peer in ep_peers:
        sends.append(
            remote(sq_s.at[peer // blocks], sq_r.at[e], sq_ss.at[peer], sq_rs.at[e], "ep", peer)
        )
        sends[-1].start()
    ffn_copies[1].wait()
    upper = jnp.dot(normed, wu_v[...], preferred_element_type=F32)
    for p in range(ne):
        some = slice(p // blocks * gr, (p // blocks + 1) * gr)
        cols = slice(p % blocks * LANES, (p % blocks + 1) * LANES)
        gu_s[p] = jnp.concatenate([gate[some, cols], upper[some, cols]], axis=1).astype(BF16)
    for peer in ep_peers:
        sends.append(remote(gu_s.at[peer], gu_r.at[e], gu_ss.at[peer], gu_rs.at[e], "ep", peer))
        sends[-1].start()
    settle()
    squares = sq_s[e // blocks].astype(F32)
    sums = gu_s[e].astype(F32)
    for src in ep_peers:
        remote(sq_s.at[0], sq_r.at[src], sq_ss.at[src], sq_rs.at[src], "ep", src).wait_recv()
        squares = squares + sq_r[src].astype(F32)
    for src in ep_peers:
        remote(gu_s.at[src], gu_r.at[src], gu_ss.at[src], gu_rs.at[src], "ep", src).wait_recv()
        sums = sums + gu_r[src].astype(F32)
    square = squares[:, :1] + squares[:, LANES // 2 : LANES // 2 + 1]
    inv_rms = lax.rsqrt(square / (dl * ne) + EPSILON)
    gate = inv_rms * sums[:, :LANES]
    upper = inv_rms * sums[:, LANES:]
    eh_r[e] = (gate / (1.0 + jnp.exp(-gate)) * upper).astype(BF16)
    for peer in ep_peers:
        sends.append(remote(eh_r.at[e], eh_r.at[e], eh_ss.at[peer], eh_rs.at[e], "ep", peer))
        sends[-1].start()
    settle()
    small_copies[3].wait()
    small_copies[4].wait()
    route = jnp.sum(jnp.where(ids_ref[...] == c, rw_ref[...], 0.0), axis=0, keepdims=True)
    diagonal = lax.broadcasted_iota(jnp.int32, (rows, rows), 0) == lax.broadcasted_iota(jnp.int32, (rows, rows), 1)
    route = jnp.sum(jnp.where(diagonal, route, 0.0), axis=1, keepdims=True)
    ffn_copies[2].wait()
    for src in ep_peers:
        remote(eh_r.at[src], eh_r.at[src], eh_ss.at[src], eh_rs.at[src], "ep", src).wait_recv()

    left = [
        jnp.concatenate([eh_r[j * blocks + b] for b in range(blocks)], axis=1) for j in range(rows // gr)
    ]
    left = jnp.concatenate(left, axis=0) if len(left) > 1 else left[0]
    expert = route * jnp.dot(left, wd_v[...], preferred_element_type=F32)
    for j in range(nc):
        mo_s[j] = expert[j * ro : (j + 1) * ro].astype(BF16)
    for peer in ctx_peers:
        sends.append(remote(mo_s.at[peer], mo_r.at[c], mo_ss.at[peer], mo_rs.at[c], "ctx", peer))
        sends[-1].start()
    settle()
    result = hid_s[c] + mo_s[c].astype(F32)
    for src in ctx_peers:
        remote(mo_s.at[src], mo_r.at[src], mo_ss.at[src], mo_rs.at[src], "ctx", src).wait_recv()
        result = result + mo_r[src].astype(F32)
    out_ref[...] = result.astype(BF16)


def local(
    nc, ne, queries, latent_cache, lengths, value_up, out_proj, residual, norm_gain,
    expert_ids, route_weight, gate_proj, up_proj, down_proj,
):
    rl, heads, width = queries.shape
    positions = latent_cache.shape[1]
    hpd = value_up.shape[0]
    ro, dl = residual.shape
    rows = expert_ids.shape[0]
    ffw = gate_proj.shape[2]
    blocks = ffw // LANES
    gr = rows * blocks // ne
    nq = hpd // GROUP
    chunks = 2 if nq % 2 == 0 else 1
    qw = nq // chunks
    wide = rl * GROUP
    cut = pl.cdiv(dl, 2 * LANES) * LANES
    vm = pltpu.VMEM
    dma = pltpu.SemaphoreType.DMA
    scratch = [
        vm((rl, width, heads), BF16),
        vm((rl, width, positions), BF16),
        vm(value_up.shape, BF16),
        vm(out_proj.shape, BF16),
        vm(gate_proj.shape[1:], BF16),
        vm(up_proj.shape[1:], BF16),
        vm(down_proj.shape[1:], BF16),
        pltpu.SMEM((rl,), jnp.int32),
        vm((ro, dl), BF16),
        vm((dl,), BF16),
        vm((expert_ids.shape[1], rows), jnp.int32),
        vm((expert_ids.shape[1], rows), F32),
        vm((nc, chunks, rl, hpd // chunks, LATENT), BF16),
        vm((nc, chunks, rl, hpd // chunks, LATENT), BF16),
        vm((nc, hpd, LANES), BF16),
        vm((nc, hpd, LANES), BF16),
        vm((chunks, ne, wide, qw * VDIM), BF16),
        vm((nc, rows, cut), BF16),
        vm((nc, rows, dl - cut), BF16),
        vm((nc, ro, dl), F32),
        vm((rows // gr, gr, LANES), BF16),
        vm((ne, gr, LANES), BF16),
        vm((ne, gr, 2 * LANES), BF16),
        vm((ne, gr, 2 * LANES), BF16),
        vm((ne, gr, LANES), BF16),
        vm((nc, ro, dl), BF16),
        vm((nc, ro, dl), BF16),
        dma((rl, 2)),
        dma((chunks,)),
        dma((chunks,)),
        dma((3,)),
        dma((5,)),
    ]
    for shape in ((nc, chunks), (nc,), (chunks, ne), (2, nc), (ne,), (ne,), (ne,), (nc,)):
        scratch += [dma(shape), dma(shape)]
    weights = value_up.size + out_proj.size + gate_proj.size + up_proj.size + down_proj.size
    return pl.pallas_call(
        functools.partial(kernel, nc, ne, chunks),
        out_shape=jax.ShapeDtypeStruct((ro, dl), BF16),
        in_specs=[pl.BlockSpec(memory_space=pl.ANY)] * 12,
        out_specs=pl.BlockSpec(memory_space=pltpu.VMEM),
        scratch_shapes=scratch,
        compiler_params=pltpu.CompilerParams(
            collective_id=0, has_side_effects=True, vmem_limit_bytes=63 * 2**20
        ),
        cost_estimate=pl.CostEstimate(
            flops=2 * rows * weights, bytes_accessed=2 * weights, transcendentals=rl * heads * positions
        ),
        name="decode_step",
    )(
        queries.transpose(0, 2, 1), latent_cache.transpose(0, 2, 1), lengths, value_up, out_proj, residual,
        norm_gain, expert_ids.T, route_weight.T, gate_proj, up_proj, down_proj,
    )


def solution(mesh):
    placed = (
        P("ep", None, None),
        P("ep", "ctx", None),
        P("ep"),
        P("ctx", None, None),
        P("ctx", "ep"),
        P("ctx", "ep"),
        P("ep"),
        P(),
        P(),
        P("ctx", "ep", None),
        P("ctx", "ep", None),
        P("ctx", None, "ep"),
    )
    step = functools.partial(local, mesh.shape["ctx"], mesh.shape["ep"])
    return jax.shard_map(step, mesh=mesh, in_specs=placed, out_specs=P("ctx", "ep"), check_vma=False)
```
